512 devices in a mesh: ia: 8 (over x, core), ja: 8 (over z_lo), ka: 8 (over z_hi, y).
Axes of the slice: x: 4, y: 4, z: 16 (z_hi: 2, z_lo: 8; z = z_hi * 8 + z_lo), core: 2. Of those that a mesh axis runs over, the one named last changes fastest.
Arguments:
- tokens: bfloat16 [2048, 4096], P('ia', ('ka', 'ja')), may hold values from -6 to 6
- weight_in: bfloat16 [4096, 16384], P('ka', ('ja', 'ia')), may hold values from -0.09375 to 0.09375
- weight_out: bfloat16 [16384, 4096], P('ja', ('ka', 'ia')), may hold values from -0.046875 to 0.046875
- cotangent: bfloat16 [2048, 4096], P('ia', ('ka', 'ja')), may hold values from -6 to 6
- row_mask: int32 [2048], P('ia'), may hold values 0 or 1
Outputs:
- block_out: bfloat16 [2048, 4096], P('ia', ('ka', 'ja'))
- grad_tokens: bfloat16 [2048, 4096], P('ia', ('ka', 'ja'))
The draws below stay inside these ranges and needn't reach their ends.
All inputs are finite; a program needn't handle non-finite values. No bound on the sum of `row_mask` on one device may be relied on, other than what follows from the above.
Results may differ from the reference program's by a relative error of at most 0.02.
Values may be sent and summed in bfloat16 or wider, within the bound.
No kernel may reach another device: no remote copies, remote signals or barrier semaphores. Data moves between devices by JAX's collectives and lax.ppermute only.
A program may use at most 64 MiB of HBM per device.

```python
import jax
import jax.numpy as jnp
from jax import lax

D = 4096
FF = 16384
TOKENS = 2048
N_JA = 8
N_KA = 8


def set_ends(drawn, own_key, smallest, largest):
    extent = drawn.shape
    place = [jax.random.randint(jax.random.fold_in(own_key, axis), (), 0, extent[axis]) for axis in range(len(extent))]
    drawn = drawn.at[tuple(place)].set(smallest)
    longest = extent.index(max(extent))
    place[longest] = (place[longest] + 1) % extent[longest]
    return drawn.at[tuple(place)].set(largest)


def steps_of(own_key, extent, shards, low, high):
    loudness, own = 1.0, jax.random.fold_in(own_key, 6)
    for axis_at, parts in shards:
        draws = jnp.exp(jax.random.uniform(jax.random.fold_in(own, axis_at), (parts,), jnp.float32, low / len(shards), high / len(shards)))
        loudness = loudness * jnp.repeat(draws, extent[axis_at] // parts).reshape([-1 if axis == axis_at else 1 for axis in range(len(extent))])
    return loudness


def centred(stream_key, extent, scale, bound, split=(), held_as=jnp.bfloat16):
    entries = scale * jax.random.normal(stream_key, extent, jnp.float32)
    if split:
        entries = entries * steps_of(stream_key, extent, split, -0.22, 0.18)
    return jnp.clip(entries, -bound, bound).astype(held_as)


def setup_inputs(seed: int = 0) -> dict:
    arg_keys = jax.random.split(jax.random.key(seed), 6)
    return {
        "tokens": centred(arg_keys[0], (TOKENS, D), 1.0, 6.0, ((0, 8), (1, 64))),
        "weight_in": centred(arg_keys[1], (D, FF), D ** -0.5, 0.09375, ((0, 8), (1, 64))),
        "weight_out": centred(arg_keys[2], (FF, D), FF ** -0.5, 0.046875, ((0, 8), (1, 64))),
        "cotangent": centred(arg_keys[3], (TOKENS, D), 1.0, 6.0, ((0, 8), (1, 64))),
        "row_mask": set_ends((jax.random.randint(arg_keys[4], (TOKENS,), 0, 2) < 1).astype(jnp.int32), jax.random.fold_in(arg_keys[4], 1), 0, 1),
    }


gelu_coef = 0.7978845608028654


def gelu_value(preact):
    inner = gelu_coef * (preact + 0.044715 * preact * preact * preact)
    return 0.5 * preact * (1.0 + jnp.tanh(inner))


def gelu_slope(preact):
    inner = gelu_coef * (preact + 0.044715 * preact * preact * preact)
    tangent = jnp.tanh(inner)
    return 0.5 * (1.0 + tangent) + 0.5 * preact * (1.0 - tangent * tangent) * gelu_coef * (1.0 + 3.0 * 0.044715 * preact * preact)


def block_product(left, right, blocks, transposed):
    width = left.shape[1] // blocks
    out_cols = right.shape[0] if transposed else right.shape[1]

    def add_block(index, summed):
        offset = (index * width).astype(jnp.int32)
        left_part = lax.dynamic_slice_in_dim(left, offset, width, 1)
        if transposed:
            right_part = lax.dynamic_slice_in_dim(right, offset, width, 1)
            term = lax.dot_general(left_part, right_part, (((1,), (1,)), ((), ())), preferred_element_type=jnp.float32)
        else:
            right_part = lax.dynamic_slice_in_dim(right, offset, width, 0)
            term = jnp.dot(left_part, right_part, preferred_element_type=jnp.float32)
        rounded = lax.optimization_barrier(term.astype(jnp.bfloat16))
        return summed + rounded.astype(jnp.float32)

    return lax.fori_loop(0, blocks, add_block, jnp.zeros((left.shape[0], out_cols), jnp.float32))


def reference(tokens, weight_in, weight_out, cotangent, row_mask):
    preact = block_product(tokens, weight_in, N_KA, False)
    hidden = gelu_value(preact).astype(jnp.bfloat16)
    branch = block_product(hidden, weight_out, N_JA, False)
    block_out = (tokens.astype(jnp.float32) + branch).astype(jnp.bfloat16)
    masked = cotangent * row_mask[:, None].astype(jnp.bfloat16)
    grad_hidden = block_product(masked, weight_out, N_KA, True)
    grad_preact = (grad_hidden * gelu_slope(preact)).astype(jnp.bfloat16)
    grad_branch = block_product(grad_preact, weight_in, N_JA, True)
    grad_tokens = (masked.astype(jnp.float32) + grad_branch).astype(jnp.bfloat16)
    return block_out, grad_tokens
```

```python
import jax
import jax.numpy as jnp
from jax import lax
from jax.experimental import pallas as pl
from jax.experimental.pallas import tpu as pltpu
from jax.sharding import Mesh, PartitionSpec as P

gelu_coef = 0.7978845608028654

AXES = ("x", "core", "quad", "place", "half", "y")
SIZES = (4, 2, 2, 4, 2, 4)
IA, JA, KA = ("x", "core"), ("quad", "place"), ("half", "y")
QUADS = ("half", "quad")

VMEM = pl.BlockSpec(memory_space=pltpu.VMEM)
PARAMS = pltpu.CompilerParams(vmem_limit_bytes=48 * 2**20)


def exchange(parts, axis):
    return lax.all_to_all(parts, axis, split_axis=0, concat_axis=0, tiled=True)


def spread(shard, axis, size):
    return exchange(jnp.broadcast_to(shard[None], (size,) + shard.shape), axis)


def gelu_both(preact):
    inner = gelu_coef * (preact + 0.044715 * preact * preact * preact)
    tangent = jnp.tanh(inner)
    value = 0.5 * preact * (1.0 + tangent)
    slope = 0.5 * (1.0 + tangent) + 0.5 * preact * (1.0 - tangent * tangent) * gelu_coef * (
        1.0 + 3.0 * 0.044715 * preact * preact
    )
    return value, slope


def whole_in(weights):
    return jnp.concatenate(
        [
            jnp.concatenate([weights[core, x, half, 0] for x in range(4) for core in range(2)], axis=1)
            for half in range(2)
        ],
        axis=0,
    )


def whole_out(weights):
    return jnp.concatenate(
        [
            jnp.concatenate([weights[core, x, half, 1, 64 * q : 64 * q + 64] for q in range(8)], axis=1)
            for half in range(2)
            for x in range(4)
            for core in range(2)
        ],
        axis=0,
    )


def first_kernel(inputs, weights, terms):
    for which, whole in ((0, whole_in), (1, whole_out)):
        block = jnp.concatenate(
            [inputs[place, group, which] for group in range(4) for place in range(4)], axis=0
        )
        full = whole(weights)
        product = lax.dot_general(full, block, (((0,), (0,)), ((), ())), preferred_element_type=jnp.float32)
        for part in range(4):
            terms[part, which] = product[256 * part : 256 * part + 256].astype(jnp.bfloat16)


def middle_kernel(terms, hidden):
    preact = sum(terms[part, 0].astype(jnp.float32) for part in range(4))
    grad = sum(terms[part, 1].astype(jnp.float32) for part in range(4))
    value, slope = gelu_both(preact)
    value = value.astype(jnp.bfloat16)
    grad = (grad * slope).astype(jnp.bfloat16)
    for part in range(4):
        hidden[part, 0] = value
        hidden[part, 1] = grad


def second_kernel(hidden, weights, terms):
    for which, whole in ((0, whole_out), (1, whole_in)):
        block = jnp.concatenate([hidden[part, which] for part in range(4)], axis=0)
        product = jnp.dot(whole(weights), block, preferred_element_type=jnp.float32).astype(jnp.bfloat16)
        for group in range(4):
            for place in range(4):
                start = 256 * group + 64 * place
                terms[place, group, which] = product[start : start + 64]


def call(kernel, shape, *operands):
    return pl.pallas_call(
        kernel,
        out_shape=jax.ShapeDtypeStruct(shape, jnp.bfloat16),
        in_specs=[VMEM] * len(operands),
        out_specs=VMEM,
        compiler_params=PARAMS,
    )(*operands)


def shards(tokens, weight_in, weight_out, cotangent, row_mask):
    masked = cotangent * row_mask[:, None].astype(jnp.bfloat16)
    own = jnp.stack([tokens.T, masked.T])
    packed = jnp.stack(
        [
            weight_in.reshape(512, 2, 128).transpose(1, 0, 2),
            weight_out.T.reshape(64, 8, 2, 128).transpose(2, 1, 0, 3).reshape(2, 512, 128),
        ],
        axis=1,
    )
    weights = exchange(packed, "half")
    weights = spread(weights, "x", 4)
    weights = spread(weights, "core", 2)
    inputs = spread(own, QUADS, 4)
    inputs = spread(inputs, "place", 4)
    terms = call(first_kernel, (4, 2, 256, 256), inputs, weights)
    hidden = call(middle_kernel, (4, 2, 256, 256), exchange(terms, "y"))
    hidden = exchange(hidden, "y")
    terms = call(second_kernel, (4, 4, 2, 64, 256), hidden, weights)
    terms = exchange(terms, "place").astype(jnp.float32).sum(0).astype(jnp.bfloat16)
    terms = exchange(terms, QUADS).astype(jnp.float32).sum(0)
    outs = (own.astype(jnp.float32) + terms).astype(jnp.bfloat16)
    return outs[0].T, outs[1].T


def solution(mesh):
    return jax.shard_map(
        shards,
        mesh=Mesh(mesh.devices.reshape(SIZES), AXES),
        in_specs=(P(IA, KA + JA), P(KA, JA + IA), P(JA, KA + IA), P(IA, KA + JA), P(IA)),
        out_specs=(P(IA, KA + JA), P(IA, KA + JA)),
        check_vma=False,
    )
```

```python
import jax
import jax.numpy as jnp
from jax import lax
from jax.experimental import pallas as pl
from jax.experimental.pallas import tpu as pltpu
from jax.sharding import Mesh, PartitionSpec as P

gelu_coef = 0.7978845608028654

AXES = ("x", "core", "quad", "place", "half", "y")
SIZES = (4, 2, 2, 4, 2, 4)
IA, JA, KA = ("x", "core"), ("quad", "place"), ("half", "y")
QUADS = ("half", "quad")
ALONG_Z = ("quad", "place", "half")

VMEM = pl.BlockSpec(memory_space=pltpu.VMEM)
SMEM = pl.BlockSpec(memory_space=pltpu.SMEM)
BF16, F32 = jnp.bfloat16, jnp.float32


def exchange(parts, axis):
    return lax.all_to_all(parts, axis, split_axis=0, concat_axis=0, tiled=True)


def spread(shard, axis, size):
    return exchange(jnp.broadcast_to(shard[None], (size,) + shard.shape), axis)


def swap(block, axis):
    return lax.ppermute(block, axis, [(0, 1), (1, 0)])


def along_z(block, distance):
    index = lambda z: (z % 8) * 2 + z // 8
    return lax.ppermute(block, ALONG_Z, [(index(z), index((z + distance) % 16)) for z in range(16)])


def gelu_both(preact):
    inner = gelu_coef * (preact + 0.044715 * preact * preact * preact)
    tangent = jnp.tanh(inner)
    value = 0.5 * preact * (1.0 + tangent)
    slope = 0.5 * (1.0 + tangent) + 0.5 * preact * (1.0 - tangent * tangent) * gelu_coef * (
        1.0 + 3.0 * 0.044715 * preact * preact
    )
    return value, slope


def fetch(refs, held, arrived):
    copies = [pltpu.make_async_copy(ref, to, arrived.at[i]) for i, (ref, to) in enumerate(zip(refs, held))]
    for copy in copies:
        copy.start()
    for copy in copies:
        copy.wait()


def pick_half(half, weight_in, weight_out, in_part, out_part):
    in_part[...] = weight_in[:, 128 * half : 128 * half + 128]
    for q in range(8):
        start = 256 * q + 128 * half
        out_part[64 * q : 64 * q + 64] = weight_out[:, start : start + 128]


def split_kernel(where, *refs):
    operands, (rows, up, down), held, arrived = refs[:5], refs[5:8], refs[8:13], refs[13]
    fetch(operands, held, arrived)
    tokens, cotangent, row_mask, weight_in, weight_out = held
    rows[0] = tokens[...]
    rows[1] = cotangent[...] * row_mask[...].astype(BF16)
    for half in range(2):

        @pl.when(where[0] == half)
        def _():
            pick_half(half, weight_in, weight_out, up.at[:512], up.at[512:1024])
            pick_half(1 - half, weight_in, weight_out, down.at[:512], down.at[512:1024])

    for out in (up, down):
        for which in range(2):
            for lanes in range(2):
                start = 1024 + 128 * which + 64 * lanes
                out[start : start + 64] = rows[which, :, 128 * lanes : 128 * lanes + 128]


def join_kernel(below, above, blocks, next_rows, last_rows):
    for x in range(4):
        blocks[x, :1024] = below[:1024]
        blocks[x, 1024:] = above[:1024]
    for out, came in ((next_rows, above), (last_rows, below)):
        for which in range(2):
            for lanes in range(2):
                start = 1024 + 128 * which + 64 * lanes
                out[which, :, 128 * lanes : 128 * lanes + 128] = came[start : start + 64]


def rows_kernel(where, same, ahead, behind, far_a, far_b, rows):
    blocks = [(offset, quad, block, quad) for offset, block in ((0, same), (1, ahead), (15, behind)) for quad in range(4)]
    blocks += [(2, 0, far_a, 0), (2, 1, far_a, 1), (14, 3, far_b, 0), (14, 0, far_b, 1)]
    for offset, quad, block, slot in blocks:
        start = lax.rem(where[1] + offset + 4 * quad, 16)
        for which in range(2):
            rows[which, pl.ds(pl.multiple_of(64 * start, 64), 64)] = block[slot, which]


def first_kernel(where, rows, blocks, core_blocks, weights, terms):
    half, core = lax.div(lax.rem(where[1] + 12, 16), 8), where[2]
    for block, at_core in ((blocks, core), (core_blocks, 1 - core)):
        for at, at_half in ((0, half), (1024, 1 - half)):
            for x in range(4):
                lanes = pl.ds(pl.multiple_of(256 * x + 128 * at_core, 128), 128)
                weights[0, pl.ds(pl.multiple_of(512 * at_half, 512), 512), lanes] = block[x, at : at + 512]
                part = pl.ds(pl.multiple_of(512 * at_half + 128 * x + 64 * at_core, 64), 64)
                for q in range(8):
                    start = at + 512 + 64 * q
                    weights[1, part, 128 * q : 128 * q + 128] = block[x, start : start + 64]
    for which in range(2):
        product = lax.dot_general(
            weights[which], rows[which], (((0,), (0,)), ((), ())), preferred_element_type=F32
        )
        for part in range(4):
            terms[part, which] = product[256 * part : 256 * part + 256].astype(BF16)


def middle_kernel(terms, hidden):
    preact = sum(terms[part, 0].astype(F32) for part in range(4))
    grad = sum(terms[part, 1].astype(F32) for part in range(4))
    value, slope = gelu_both(preact)
    value = value.astype(BF16)
    grad = (grad * slope).astype(BF16)
    for part in range(4):
        hidden[part, 0] = value
        hidden[part, 1] = grad


def second_kernel(where, hidden, weights, same, ahead, behind, far_a, far_b, rows):
    place = lax.rem(where[1], 4)
    for which in range(2):
        block = jnp.concatenate([hidden[part, which] for part in range(4)], axis=0)
        rows[which] = jnp.dot(weights[1 - which], block, preferred_element_type=F32).astype(BF16)
    for group in range(4):
        for which in range(2):
            for offset, out, slot in (
                (0, same, group),
                (1, ahead, group),
                (3, behind, group),
                (2, far_a if group < 2 else far_b, group % 2),
            ):
                at = lax.rem(place + offset, 4)
                out[slot, which] = rows[which, pl.ds(pl.multiple_of(256 * group + 64 * at, 64), 64)]


def call(kernel, shapes, *operands, scratch=(), space=VMEM, mib=20):
    return pl.pallas_call(
        kernel,
        out_shape=[jax.ShapeDtypeStruct(shape, BF16) for shape in shapes],
        in_specs=[SMEM if operand.dtype == jnp.int32 and operand.shape == (3,) else space for operand in operands],
        out_specs=[VMEM] * len(shapes),
        scratch_shapes=[pltpu.VMEM(shape, BF16) if isinstance(shape, tuple) else shape for shape in scratch],
        compiler_params=pltpu.CompilerParams(vmem_limit_bytes=mib * 2**20),
    )(*operands)


def shards(tokens, weight_in, weight_out, cotangent, row_mask):
    half = lax.axis_index("half")
    at_z = 8 * half + 4 * lax.axis_index("quad") + lax.axis_index("place")
    where = jnp.stack([half, at_z, lax.axis_index("core")]).astype(jnp.int32)
    weights = (weight_in, weight_out.T)
    operands = (tokens.T, cotangent.T, row_mask[None]) + weights
    held = lambda arrays: [pltpu.VMEM(a.shape, a.dtype) for a in arrays] + [pltpu.SemaphoreType.DMA((len(arrays),))]
    outside = pl.BlockSpec(memory_space=pl.ANY)
    own, up, down = call(
        split_kernel, [(2, 64, 256), (1280, 128), (1280, 128)], where, *operands,
        scratch=held(operands), space=outside, mib=60,
    )
    blocks, next_rows, last_rows = call(
        join_kernel, [(4, 2048, 128), (2, 64, 256), (2, 64, 256)], along_z(up, 4), along_z(down, -4)
    )
    blocks = exchange(blocks, "x")
    same = jnp.stack([own, next_rows, along_z(next_rows, -4), last_rows])
    behind, ahead = along_z(same, 1), along_z(same, -1)
    far_a, far_b = along_z(same[:2], -2), along_z(jnp.stack([last_rows, own]), 2)
    (rows,) = call(rows_kernel, [(2, 1024, 256)], where, same, ahead, behind, far_a, far_b)
    blocks, rows = lax.optimization_barrier((blocks, rows))
    core_blocks = swap(blocks, "core")
    weights, terms = call(
        first_kernel, [(2, 1024, 1024), (4, 2, 256, 256)], where, rows, blocks, core_blocks
    )
    (hidden,) = call(middle_kernel, [(4, 2, 256, 256)], exchange(terms, "y"))
    hidden = exchange(hidden, "y")
    whole, part = (4, 2, 64, 256), (2, 2, 64, 256)
    same, ahead, behind, far_a, far_b = call(
        second_kernel, [whole, whole, whole, part, part], where, hidden, weights, scratch=[(2, 1024, 256)]
    )
    sums = [along_z(ahead, 1), along_z(behind, -1), jnp.concatenate([along_z(far_a, 2), along_z(far_b, -2)])]
    terms = same.astype(F32) + sum(block.astype(F32) for block in sums)
    terms = exchange(terms.astype(BF16), QUADS).astype(F32).sum(0)
    outs = (own.astype(F32) + terms).astype(BF16)
    return outs[0].T, outs[1].T


def solution(mesh):
    return jax.shard_map(
        shards,
        mesh=Mesh(mesh.devices.reshape(SIZES), AXES),
        in_specs=(P(IA, KA + JA), P(KA, JA + IA), P(JA, KA + IA), P(IA, KA + JA), P(IA)),
        out_specs=(P(IA, KA + JA), P(IA, KA + JA)),
        check_vma=False,
    )
```

```python
import jax
import jax.numpy as jnp
from jax import lax
from jax.experimental import pallas as pl
from jax.experimental.pallas import tpu as pltpu
from jax.sharding import Mesh, PartitionSpec as P

gelu_coef = 0.7978845608028654

AXES = ("x", "core", "quad", "place", "half", "y")
SIZES = (4, 2, 2, 4, 2, 4)
IA, JA, KA = ("x", "core"), ("quad", "place"), ("half", "y")
QUADS = ("half", "quad")
ALONG_Z = ("quad", "place", "half")

VMEM = pl.BlockSpec(memory_space=pltpu.VMEM)
BF16, F32 = jnp.bfloat16, jnp.float32
COST = 5 * 10**10


def exchange(parts, axis):
    return lax.all_to_all(parts, axis, split_axis=0, concat_axis=0, tiled=True)


def spread(shard, axis, size):
    return exchange(jnp.broadcast_to(shard[None], (size,) + shard.shape), axis)


def swap(block, axis):
    return lax.ppermute(block, axis, [(0, 1), (1, 0)])


def along_z(block, distance):
    index = lambda z: (z % 8) * 2 + z // 8
    return lax.ppermute(block, ALONG_Z, [(index(z), index((z + distance) % 16)) for z in range(16)])


def place_on_z():
    return 8 * lax.axis_index("half") + 4 * lax.axis_index("quad") + lax.axis_index("place")


def gelu_both(preact):
    inner = gelu_coef * (preact + 0.044715 * preact * preact * preact)
    tangent = jnp.tanh(inner)
    value = 0.5 * preact * (1.0 + tangent)
    slope = 0.5 * (1.0 + tangent) + 0.5 * preact * (1.0 - tangent * tangent) * gelu_coef * (
        1.0 + 3.0 * 0.044715 * preact * preact
    )
    return value, slope


def fetch(refs, held, arrived):
    copies = [pltpu.make_async_copy(ref, to, arrived.at[i]) for i, (ref, to) in enumerate(zip(refs, held))]
    for copy in copies:
        copy.start()
    for copy in copies:
        copy.wait()


def pick_half(half, weight_in, weight_out, in_part, out_part):
    in_part[...] = weight_in[:, 128 * half : 128 * half + 128]
    for q in range(8):
        start = 256 * q + 128 * half
        out_part[64 * q : 64 * q + 64] = weight_out[:, start : start + 128]


def split_kernel(*refs):
    operands, (rows, up, down), held, arrived = refs[:5], refs[5:8], refs[8:13], refs[13]
    fetch(operands, held, arrived)
    tokens, cotangent, row_mask, weight_in, weight_out = held
    rows[0] = tokens[...]
    rows[1] = cotangent[...] * row_mask[...].astype(BF16)
    for half in range(2):

        @pl.when(lax.axis_index("half") == half)
        def _():
            pick_half(half, weight_in, weight_out, up.at[:512], up.at[512:1024])
            pick_half(1 - half, weight_in, weight_out, down.at[:512], down.at[512:1024])

    for out in (up, down):
        for which in range(2):
            for lanes in range(2):
                start = 1024 + 128 * which + 64 * lanes
                out[start : start + 64] = rows[which, :, 128 * lanes : 128 * lanes + 128]


def join_kernel(below, above, blocks, next_rows, last_rows, moved):
    copies = []
    for x in range(4):
        for at, came in ((0, below), (1024, above)):
            copies.append(pltpu.make_async_copy(came.at[:1024], blocks.at[x, at : at + 1024], moved.at[len(copies)]))
    for out, came in ((next_rows, above), (last_rows, below)):
        for which in range(2):
            for lanes in range(2):
                start = 1024 + 128 * which + 64 * lanes
                part = out.at[which, :, 128 * lanes : 128 * lanes + 128]
                copies.append(pltpu.make_async_copy(came.at[start : start + 64], part, moved.at[len(copies)]))
    for copy in copies:
        copy.start()
    for copy in copies:
        copy.wait()


def lay_rows(rows, same, ahead, behind, far_a, far_b):
    at_z = place_on_z()
    blocks = [(offset, quad, block, quad) for offset, block in ((0, same), (1, ahead), (15, behind)) for quad in range(4)]
    blocks += [(2, 0, far_a, 0), (2, 1, far_a, 1), (14, 3, far_b, 0), (14, 0, far_b, 1)]
    for offset, quad, block, slot in blocks:
        start = lax.rem(at_z + offset + 4 * quad, 16)
        for which in range(2):
            rows[which, pl.ds(pl.multiple_of(64 * start, 64), 64)] = block[slot, which]


def lay_weights(weights, block, at_core):
    half = lax.div(lax.rem(place_on_z() + 12, 16), 8)
    for at, at_half in ((0, half), (1024, 1 - half)):
        for x in range(4):
            lanes = pl.ds(pl.multiple_of(256 * x + 128 * at_core, 128), 128)
            weights[0, pl.ds(pl.multiple_of(512 * at_half, 512), 512), lanes] = block[x, at : at + 512]
            part = pl.ds(pl.multiple_of(512 * at_half + 128 * x + 64 * at_core, 64), 64)
            for q in range(8):
                start = at + 512 + 64 * q
                weights[1, part, 128 * q : 128 * q + 128] = block[x, start : start + 64]


def own_kernel(same, ahead, behind, far_a, far_b, blocks, rows, weights):
    lay_rows(rows, same, ahead, behind, far_a, far_b)
    lay_weights(weights, blocks, lax.axis_index("core"))


def first_kernel(rows, begun, core_blocks, weights, terms):
    lay_weights(weights, core_blocks, 1 - lax.axis_index("core"))
    for which in range(2):
        product = lax.dot_general(
            rows[which], weights[which], (((0,), (0,)), ((), ())), preferred_element_type=F32
        )
        for part in range(4):
            terms[part, which] = product[:, 256 * part : 256 * part + 256].astype(BF16)


def middle_kernel(terms, hidden):
    preact = sum(terms[part, 0].astype(F32) for part in range(4))
    grad = sum(terms[part, 1].astype(F32) for part in range(4))
    value, slope = gelu_both(preact)
    value = value.astype(BF16)
    grad = (grad * slope).astype(BF16)
    for part in range(4):
        hidden[part, 0] = value
        hidden[part, 1] = grad


def second_kernel(hidden, weights, same, ahead, behind, far_a, far_b, rows):
    place = lax.axis_index("place")
    for which in range(2):
        block = jnp.concatenate([hidden[part, which] for part in range(4)], axis=1)
        product = lax.dot_general(
            weights[1 - which], block, (((1,), (1,)), ((), ())), preferred_element_type=F32
        )
        rows[which] = product.astype(BF16)
    for group in range(4):
        for which in range(2):
            for offset, out, slot in (
                (0, same, group),
                (1, ahead, group),
                (3, behind, group),
                (2, far_a if group < 2 else far_b, group % 2),
            ):
                at = lax.rem(place + offset, 4)
                out[slot, which] = rows[which, pl.ds(pl.multiple_of(256 * group + 64 * at, 64), 64)]


def call(kernel, shapes, *operands, scratch=(), space=VMEM, out_space=VMEM, mib=20, aliases={}, cost=None):
    return pl.pallas_call(
        kernel,
        out_shape=[jax.ShapeDtypeStruct(shape, BF16) for shape in shapes],
        in_specs=[space] * len(operands),
        out_specs=[out_space] * len(shapes),
        scratch_shapes=[pltpu.VMEM(shape, BF16) if isinstance(shape, tuple) else shape for shape in scratch],
        input_output_aliases=aliases,
        cost_estimate=pl.CostEstimate(flops=cost, bytes_accessed=0, transcendentals=0) if cost else None,
        compiler_params=pltpu.CompilerParams(vmem_limit_bytes=mib * 2**20),
    )(*operands)


def shards(tokens, weight_in, weight_out, cotangent, row_mask):
    weights = (weight_in, weight_out.T)
    operands = (tokens.T, cotangent.T, row_mask[None]) + weights
    held = lambda arrays: [pltpu.VMEM(a.shape, a.dtype) for a in arrays] + [pltpu.SemaphoreType.DMA((len(arrays),))]
    outside = pl.BlockSpec(memory_space=pl.ANY)
    own, up, down = call(
        split_kernel, [(2, 64, 256), (1280, 128), (1280, 128)], *operands,
        scratch=held(operands), space=outside, mib=60,
    )
    blocks, next_rows, last_rows = call(
        join_kernel, [(4, 2048, 128), (2, 64, 256), (2, 64, 256)], along_z(up, 4), along_z(down, -4),
        scratch=[pltpu.SemaphoreType.DMA((16,))], space=outside, out_space=outside,
    )
    blocks = exchange(blocks, "x")
    same = jnp.stack([own, next_rows, along_z(next_rows, -4), last_rows])
    behind, ahead = along_z(same, 1), along_z(same, -1)
    far_a, far_b = along_z(same[:2], -2), along_z(jnp.stack([last_rows, own]), 2)
    rows, begun = call(
        own_kernel, [(2, 1024, 256), (2, 1024, 1024)], same, ahead, behind, far_a, far_b, blocks, cost=COST
    )
    weights, terms = call(
        first_kernel,
        [(2, 1024, 1024), (4, 2, 256, 256)],
        rows, begun, swap(blocks, "core"),
        aliases={1: 0},
    )
    (hidden,) = call(middle_kernel, [(4, 2, 256, 256)], exchange(terms, "y"))
    hidden = exchange(hidden, "y")
    whole, part = (4, 2, 64, 256), (2, 2, 64, 256)
    same, ahead, behind, far_a, far_b = call(
        second_kernel, [whole, whole, whole, part, part], hidden, weights, scratch=[(2, 1024, 256)]
    )
    sums = [along_z(ahead, 1), along_z(behind, -1), jnp.concatenate([along_z(far_a, 2), along_z(far_b, -2)])]
    terms = same.astype(F32) + sum(block.astype(F32) for block in sums)
    terms = exchange(terms.astype(BF16), QUADS).astype(F32).sum(0)
    outs = (own.astype(F32) + terms).astype(BF16)
    return outs[0].T, outs[1].T


def solution(mesh):
    return jax.shard_map(
        shards,
        mesh=Mesh(mesh.devices.reshape(SIZES), AXES),
        in_specs=(P(IA, KA + JA), P(KA, JA + IA), P(JA, KA + IA), P(IA, KA + JA), P(IA)),
        out_specs=(P(IA, KA + JA), P(IA, KA + JA)),
        check_vma=False,
    )
```

```python
import jax
import jax.numpy as jnp
from jax import lax
from jax.experimental import pallas as pl
from jax.experimental.pallas import tpu as pltpu
from jax.sharding import Mesh, PartitionSpec as P

gelu_coef = 0.7978845608028654

AXES = ("x", "core", "quad", "place", "half", "y")
SIZES = (4, 2, 2, 4, 2, 4)
IA, JA, KA = ("x", "core"), ("quad", "place"), ("half", "y")
QUADS = ("half", "quad")
ALONG_Z = ("quad", "place", "half")

VMEM = pl.BlockSpec(memory_space=pltpu.VMEM)
BF16, F32 = jnp.bfloat16, jnp.float32
COST = 5 * 10**10


def exchange(parts, axis):
    return lax.all_to_all(parts, axis, split_axis=0, concat_axis=0, tiled=True)


def spread(shard, axis, size):
    return exchange(jnp.broadcast_to(shard[None], (size,) + shard.shape), axis)


def swap(block, axis):
    return lax.ppermute(block, axis, [(0, 1), (1, 0)])


def along_z(block, distance):
    index = lambda z: (z % 8) * 2 + z // 8
    return lax.ppermute(block, ALONG_Z, [(index(z), index((z + distance) % 16)) for z in range(16)])


def place_on_z():
    return 8 * lax.axis_index("half") + 4 * lax.axis_index("quad") + lax.axis_index("place")


def gelu_both(preact):
    inner = gelu_coef * (preact + 0.044715 * preact * preact * preact)
    tangent = jnp.tanh(inner)
    value = 0.5 * preact * (1.0 + tangent)
    slope = 0.5 * (1.0 + tangent) + 0.5 * preact * (1.0 - tangent * tangent) * gelu_coef * (
        1.0 + 3.0 * 0.044715 * preact * preact
    )
    return value, slope


def fetch(refs, held, arrived):
    copies = [pltpu.make_async_copy(ref, to, arrived.at[i]) for i, (ref, to) in enumerate(zip(refs, held))]
    for copy in copies:
        copy.start()
    for copy in copies:
        copy.wait()


def pick_half(half, weight_in, weight_out, in_part, out_part):
    in_part[...] = weight_in[:, 128 * half : 128 * half + 128]
    for q in range(8):
        start = 256 * q + 128 * half
        out_part[64 * q : 64 * q + 64] = weight_out[:, start : start + 128]


def split_kernel(*refs):
    operands, (rows, up, down), held, arrived = refs[:5], refs[5:8], refs[8:13], refs[13]
    fetch(operands, held, arrived)
    tokens, cotangent, row_mask, weight_in, weight_out = held
    rows[0] = tokens[...]
    rows[1] = cotangent[...] * row_mask[...].astype(BF16)
    for half in range(2):

        @pl.when(lax.axis_index("half") == half)
        def _():
            pick_half(half, weight_in, weight_out, up.at[:512], up.at[512:1024])
            pick_half(1 - half, weight_in, weight_out, down.at[:512], down.at[512:1024])

    for out in (up, down):
        for which in range(2):
            for lanes in range(2):
                start = 1024 + 128 * which + 64 * lanes
                out[start : start + 64] = rows[which, :, 128 * lanes : 128 * lanes + 128]


def join_kernel(below, above, blocks, next_rows, last_rows, moved):
    copies = []
    for x in range(4):
        for at, came in ((0, below), (1024, above)):
            copies.append(pltpu.make_async_copy(came.at[:1024], blocks.at[x, at : at + 1024], moved.at[len(copies)]))
    for out, came in ((next_rows, above), (last_rows, below)):
        for which in range(2):
            for lanes in range(2):
                start = 1024 + 128 * which + 64 * lanes
                part = out.at[which, :, 128 * lanes : 128 * lanes + 128]
                copies.append(pltpu.make_async_copy(came.at[start : start + 64], part, moved.at[len(copies)]))
    for copy in copies:
        copy.start()
    for copy in copies:
        copy.wait()


def lay_rows(rows, same, ahead, behind, far):
    at_z = place_on_z()
    for offset, block in ((0, same), (1, ahead), (2, far), (15, behind)):
        for quad in range(4):
            start = lax.rem(at_z + offset + 4 * quad, 16)
            for which in range(2):
                rows[which, pl.ds(pl.multiple_of(64 * start, 64), 64)] = block[quad, which]


def lay_weights(weights, block, at_core):
    half = lax.div(lax.rem(place_on_z() + 12, 16), 8)
    for at, at_half in ((0, half), (1024, 1 - half)):
        for x in range(4):
            lanes = pl.ds(pl.multiple_of(256 * x + 128 * at_core, 128), 128)
            weights[0, pl.ds(pl.multiple_of(512 * at_half, 512), 512), lanes] = block[x, at : at + 512]
            part = pl.ds(pl.multiple_of(512 * at_half + 128 * x + 64 * at_core, 64), 64)
            for q in range(8):
                start = at + 512 + 64 * q
                weights[1, part, 128 * q : 128 * q + 128] = block[x, start : start + 64]


def rows_kernel(same, ahead, behind, far, _, rows):
    lay_rows(rows, same, ahead, behind, far)


def first_kernel(rows, blocks, core_blocks, weights, terms):
    core = lax.axis_index("core")
    lay_weights(weights, blocks, core)
    lay_weights(weights, core_blocks, 1 - core)
    for which in range(2):
        product = lax.dot_general(
            rows[which], weights[which], (((0,), (0,)), ((), ())), preferred_element_type=F32
        )
        for part in range(4):
            terms[part, which] = product[:, 256 * part : 256 * part + 256].astype(BF16)


def middle_kernel(terms, hidden):
    preact = sum(terms[part, 0].astype(F32) for part in range(4))
    grad = sum(terms[part, 1].astype(F32) for part in range(4))
    value, slope = gelu_both(preact)
    value = value.astype(BF16)
    grad = (grad * slope).astype(BF16)
    for part in range(4):
        hidden[part, 0] = value
        hidden[part, 1] = grad


def second_kernel(hidden, weights, same, ahead, behind, far_a, far_b, rows):
    place = lax.axis_index("place")
    for which in range(2):
        block = jnp.concatenate([hidden[part, which] for part in range(4)], axis=1)
        product = lax.dot_general(
            weights[1 - which], block, (((1,), (1,)), ((), ())), preferred_element_type=F32
        )
        rows[which] = product.astype(BF16)
    for group in range(4):
        for which in range(2):
            for offset, out, slot in (
                (0, same, group),
                (1, ahead, group),
                (3, behind, group),
                (2, far_a if group < 2 else far_b, group % 2),
            ):
                at = lax.rem(place + offset, 4)
                out[slot, which] = rows[which, pl.ds(pl.multiple_of(256 * group + 64 * at, 64), 64)]


def call(kernel, shapes, *operands, scratch=(), space=VMEM, out_space=VMEM, mib=20, cost=None):
    return pl.pallas_call(
        kernel,
        out_shape=[jax.ShapeDtypeStruct(shape, BF16) for shape in shapes],
        in_specs=[space] * len(operands),
        out_specs=[out_space] * len(shapes),
        scratch_shapes=[pltpu.VMEM(shape, BF16) if isinstance(shape, tuple) else shape for shape in scratch],
        cost_estimate=pl.CostEstimate(flops=cost, bytes_accessed=0, transcendentals=0) if cost else None,
        compiler_params=pltpu.CompilerParams(vmem_limit_bytes=mib * 2**20),
    )(*operands)


def shards(tokens, weight_in, weight_out, cotangent, row_mask):
    weights = (weight_in, weight_out.T)
    operands = (tokens.T, cotangent.T, row_mask[None]) + weights
    held = lambda arrays: [pltpu.VMEM(a.shape, a.dtype) for a in arrays] + [pltpu.SemaphoreType.DMA((len(arrays),))]
    outside = pl.BlockSpec(memory_space=pl.ANY)
    own, up, down = call(
        split_kernel, [(2, 64, 256), (1280, 128), (1280, 128)], *operands,
        scratch=held(operands), space=outside, mib=60,
    )
    blocks, next_rows, last_rows = call(
        join_kernel, [(4, 2048, 128), (2, 64, 256), (2, 64, 256)], along_z(up, 4), along_z(down, -4),
        scratch=[pltpu.SemaphoreType.DMA((16,))], space=outside, out_space=outside,
    )
    blocks = exchange(blocks, "x")
    same = jnp.stack([own, next_rows, along_z(next_rows, -4), last_rows])
    behind, ahead = along_z(same, 1), along_z(same, -1)
    far = along_z(same, -2)
    (rows,) = call(rows_kernel, [(2, 1024, 256)], same, ahead, behind, far, blocks, cost=COST)
    weights, terms = call(
        first_kernel, [(2, 1024, 1024), (4, 2, 256, 256)], rows, blocks, swap(blocks, "core")
    )
    (hidden,) = call(middle_kernel, [(4, 2, 256, 256)], exchange(terms, "y"))
    hidden = exchange(hidden, "y")
    whole, part = (4, 2, 64, 256), (2, 2, 64, 256)
    same, ahead, behind, far_a, far_b = call(
        second_kernel, [whole, whole, whole, part, part], hidden, weights, scratch=[(2, 1024, 256)]
    )
    sums = [along_z(ahead, 1), along_z(behind, -1), jnp.concatenate([along_z(far_a, 2), along_z(far_b, -2)])]
    terms = same.astype(F32) + sum(block.astype(F32) for block in sums)
    terms = exchange(terms.astype(BF16), QUADS).astype(F32).sum(0)
    outs = (own.astype(F32) + terms).astype(BF16)
    return outs[0].T, outs[1].T


def solution(mesh):
    return jax.shard_map(
        shards,
        mesh=Mesh(mesh.devices.reshape(SIZES), AXES),
        in_specs=(P(IA, KA + JA), P(KA, JA + IA), P(JA, KA + IA), P(IA, KA + JA), P(IA)),
        out_specs=(P(IA, KA + JA), P(IA, KA + JA)),
        check_vma=False,
    )
```

```python
import jax
import jax.numpy as jnp
from jax import lax
from jax.experimental import pallas as pl
from jax.experimental.pallas import tpu as pltpu
from jax.sharding import Mesh, PartitionSpec as P

gelu_coef = 0.7978845608028654

AXES = ("x", "core", "quad", "place", "half", "y")
SIZES = (4, 2, 2, 4, 2, 4)
IA, JA, KA = ("x", "core"), ("quad", "place"), ("half", "y")
QUADS = ("half", "quad")
ALONG_Z = ("quad", "place", "half")

VMEM = pl.BlockSpec(memory_space=pltpu.VMEM)
BF16, F32 = jnp.bfloat16, jnp.float32
COST = 5 * 10**10


def exchange(parts, axis):
    return lax.all_to_all(parts, axis, split_axis=0, concat_axis=0, tiled=True)


def spread(shard, axis, size):
    return exchange(jnp.broadcast_to(shard[None], (size,) + shard.shape), axis)


def swap(block, axis):
    return lax.ppermute(block, axis, [(0, 1), (1, 0)])


def along_z(block, distance):
    index = lambda z: (z % 8) * 2 + z // 8
    return lax.ppermute(block, ALONG_Z, [(index(z), index((z + distance) % 16)) for z in range(16)])


def place_on_z():
    return 8 * lax.axis_index("half") + 4 * lax.axis_index("quad") + lax.axis_index("place")


def gelu_both(preact):
    inner = gelu_coef * (preact + 0.044715 * preact * preact * preact)
    tangent = jnp.tanh(inner)
    value = 0.5 * preact * (1.0 + tangent)
    slope = 0.5 * (1.0 + tangent) + 0.5 * preact * (1.0 - tangent * tangent) * gelu_coef * (
        1.0 + 3.0 * 0.044715 * preact * preact
    )
    return value, slope


def fetch(refs, held, arrived):
    copies = [pltpu.make_async_copy(ref, to, arrived.at[i]) for i, (ref, to) in enumerate(zip(refs, held))]
    for copy in copies:
        copy.start()
    for copy in copies:
        copy.wait()


def pick_half(half, weight_in, weight_out, in_part, out_part):
    in_part[...] = weight_in[:, 128 * half : 128 * half + 128]
    for q in range(8):
        start = 256 * q + 128 * half
        out_part[64 * q : 64 * q + 64] = weight_out[:, start : start + 128]


def split_kernel(*refs):
    operands, (rows, up, down), held, arrived = refs[:5], refs[5:8], refs[8:13], refs[13]
    fetch(operands, held, arrived)
    tokens, cotangent, row_mask, weight_in, weight_out = held
    rows[0] = tokens[...]
    rows[1] = cotangent[...] * row_mask[...].astype(BF16)
    for half in range(2):

        @pl.when(lax.axis_index("half") == half)
        def _():
            pick_half(half, weight_in, weight_out, up.at[:512], up.at[512:1024])
            pick_half(1 - half, weight_in, weight_out, down.at[:512], down.at[512:1024])

    for out in (up, down):
        for which in range(2):
            for lanes in range(2):
                start = 1024 + 128 * which + 64 * lanes
                out[start : start + 64] = rows[which, :, 128 * lanes : 128 * lanes + 128]


def join_kernel(below, above, blocks, next_rows, last_rows, moved):
    copies = []
    for x in range(4):
        for at, came in ((0, below), (1024, above)):
            copies.append(pltpu.make_async_copy(came.at[:1024], blocks.at[x, at : at + 1024], moved.at[len(copies)]))
    for out, came in ((next_rows, above), (last_rows, below)):
        for which in range(2):
            for lanes in range(2):
                start = 1024 + 128 * which + 64 * lanes
                part = out.at[which, :, 128 * lanes : 128 * lanes + 128]
                copies.append(pltpu.make_async_copy(came.at[start : start + 64], part, moved.at[len(copies)]))
    for copy in copies:
        copy.start()
    for copy in copies:
        copy.wait()


def lay_rows(rows, same, ahead, behind, far):
    at_z = place_on_z()
    for offset, block in ((0, same), (1, ahead), (2, far), (15, behind)):
        for quad in range(4):
            start = lax.rem(at_z + offset + 4 * quad, 16)
            for which in range(2):
                rows[which, pl.ds(pl.multiple_of(64 * start, 64), 64)] = block[quad, which]


def lay_share(block, ins, outs):
    half = lax.div(lax.rem(place_on_z() + 12, 16), 8)
    for at, at_half in ((0, half), (1024, 1 - half)):
        for x in range(4):
            ins[pl.ds(pl.multiple_of(512 * at_half, 512), 512), 128 * x : 128 * x + 128] = block[x, at : at + 512]
            part = pl.ds(pl.multiple_of(256 * at_half + 64 * x, 64), 64)
            for q in range(8):
                start = at + 512 + 64 * q
                outs[part, 128 * q : 128 * q + 128] = block[x, start : start + 64]


def share_of(core):
    return [pl.multiple_of(512 * half + 128 * x + 64 * core, 64) for half in range(2) for x in range(4)]


def share_products(rows, ins, outs, core):
    masked = jnp.concatenate([rows[1, pl.ds(start, 64)] for start in share_of(core)], axis=0)
    contract = (((0,), (0,)), ((), ()))
    return (
        lax.dot_general(rows[0], ins[...], contract, preferred_element_type=F32),
        lax.dot_general(masked, outs[...], contract, preferred_element_type=F32),
    )


def own_kernel(same, ahead, behind, far, block, rows, ins, outs, preact, grad):
    lay_rows(rows, same, ahead, behind, far)
    lay_share(block, ins, outs)
    own_preact, own_grad = share_products(rows, ins, outs, lax.axis_index("core"))
    preact[...] = own_preact.astype(BF16)
    grad[...] = own_grad


def first_kernel(rows, block, preact, grad, ins, outs, terms):
    core = lax.axis_index("core")
    lay_share(block, ins, outs)
    other_preact, other_grad = share_products(rows, ins, outs, 1 - core)
    other_preact = other_preact.astype(BF16)
    total = (grad[...] + other_grad).astype(BF16)
    for x in range(4):
        terms[x, 0, :, pl.ds(pl.multiple_of(128 * core, 128), 128)] = preact[:, 128 * x : 128 * x + 128]
        terms[x, 0, :, pl.ds(pl.multiple_of(128 * (1 - core), 128), 128)] = other_preact[:, 128 * x : 128 * x + 128]
        terms[x, 1] = total[:, 256 * x : 256 * x + 256]


def middle_kernel(terms, hidden):
    preact = sum(terms[part, 0].astype(F32) for part in range(4))
    grad = sum(terms[part, 1].astype(F32) for part in range(4))
    value, slope = gelu_both(preact)
    value = value.astype(BF16)
    grad = (grad * slope).astype(BF16)
    for part in range(4):
        hidden[part, 0] = value
        hidden[part, 1] = grad


def second_kernel(hidden, own_ins, own_outs, other_ins, other_outs, same, ahead, behind, far_a, far_b, rows):
    core, place = lax.axis_index("core"), lax.axis_index("place")
    contract = (((1,), (1,)), ((), ()))
    block = jnp.concatenate([hidden[x, 0] for x in range(4)], axis=1)
    grad = jnp.zeros((1024, 256), F32)
    for at_core, ins, outs in ((core, own_ins, own_outs), (1 - core, other_ins, other_outs)):
        product = lax.dot_general(outs[...], block, contract, preferred_element_type=F32).astype(BF16)
        for i, start in enumerate(share_of(at_core)):
            rows[0, pl.ds(start, 64)] = product[64 * i : 64 * i + 64]
        lanes = pl.ds(pl.multiple_of(128 * at_core, 128), 128)
        part = jnp.concatenate([hidden[x, 1, :, lanes] for x in range(4)], axis=1)
        grad += lax.dot_general(ins[...], part, contract, preferred_element_type=F32)
    rows[1] = grad.astype(BF16)
    for group in range(4):
        for which in range(2):
            for offset, out, slot in (
                (0, same, group),
                (1, ahead, group),
                (3, behind, group),
                (2, far_a if group < 2 else far_b, group % 2),
            ):
                at = lax.rem(place + offset, 4)
                out[slot, which] = rows[which, pl.ds(pl.multiple_of(256 * group + 64 * at, 64), 64)]


def call(kernel, shapes, *operands, scratch=(), space=VMEM, out_space=VMEM, mib=20, cost=None):
    return pl.pallas_call(
        kernel,
        out_shape=[jax.ShapeDtypeStruct(shape, BF16) if isinstance(shape, tuple) else shape for shape in shapes],
        in_specs=[space] * len(operands),
        out_specs=[out_space] * len(shapes),
        scratch_shapes=[pltpu.VMEM(shape, BF16) if isinstance(shape, tuple) else shape for shape in scratch],
        cost_estimate=pl.CostEstimate(flops=cost, bytes_accessed=0, transcendentals=0) if cost else None,
        compiler_params=pltpu.CompilerParams(vmem_limit_bytes=mib * 2**20),
    )(*operands)


def shards(tokens, weight_in, weight_out, cotangent, row_mask):
    weights = (weight_in, weight_out.T)
    operands = (tokens.T, cotangent.T, row_mask[None]) + weights
    held = lambda arrays: [pltpu.VMEM(a.shape, a.dtype) for a in arrays] + [pltpu.SemaphoreType.DMA((len(arrays),))]
    outside = pl.BlockSpec(memory_space=pl.ANY)
    own, up, down = call(
        split_kernel, [(2, 64, 256), (1280, 128), (1280, 128)], *operands,
        scratch=held(operands), space=outside, mib=60,
    )
    blocks, next_rows, last_rows = call(
        join_kernel, [(4, 2048, 128), (2, 64, 256), (2, 64, 256)], along_z(up, 4), along_z(down, -4),
        scratch=[pltpu.SemaphoreType.DMA((16,))], space=outside, out_space=outside,
    )
    blocks = exchange(blocks, "x")
    same = jnp.stack([own, next_rows, along_z(next_rows, -4), last_rows])
    behind, ahead = along_z(same, 1), along_z(same, -1)
    far = along_z(same, -2)
    share = [(1024, 512), (512, 1024)]
    rows, ins, outs, preact, grad = call(
        own_kernel,
        [(2, 1024, 256)] + share + [(256, 512), jax.ShapeDtypeStruct((256, 1024), F32)],
        same, ahead, behind, far, blocks,
        cost=COST,
    )
    other_ins, other_outs, terms = call(
        first_kernel, share + [(4, 2, 256, 256)], rows, swap(blocks, "core"), preact, grad
    )
    (hidden,) = call(middle_kernel, [(4, 2, 256, 256)], exchange(terms, "y"))
    hidden = exchange(hidden, "y")
    whole, part = (4, 2, 64, 256), (2, 2, 64, 256)
    same, ahead, behind, far_a, far_b = call(
        second_kernel, [whole, whole, whole, part, part], hidden, ins, outs, other_ins, other_outs,
        scratch=[(2, 1024, 256)],
    )
    sums = [along_z(ahead, 1), along_z(behind, -1), jnp.concatenate([along_z(far_a, 2), along_z(far_b, -2)])]
    terms = same.astype(F32) + sum(block.astype(F32) for block in sums)
    terms = exchange(terms.astype(BF16), QUADS).astype(F32).sum(0)
    outs = (own.astype(F32) + terms).astype(BF16)
    return outs[0].T, outs[1].T


def solution(mesh):
    return jax.shard_map(
        shards,
        mesh=Mesh(mesh.devices.reshape(SIZES), AXES),
        in_specs=(P(IA, KA + JA), P(KA, JA + IA), P(JA, KA + IA), P(IA, KA + JA), P(IA)),
        out_specs=(P(IA, KA + JA), P(IA, KA + JA)),
        check_vma=False,
    )
```

```python
import jax
import jax.numpy as jnp
from jax import lax
from jax.experimental import pallas as pl
from jax.experimental.pallas import tpu as pltpu
from jax.sharding import Mesh, PartitionSpec as P

gelu_coef = 0.7978845608028654

AXES = ("x", "core", "quad", "place", "half", "y")
SIZES = (4, 2, 2, 4, 2, 4)
IA, JA, KA = ("x", "core"), ("quad", "place"), ("half", "y")
QUADS = ("half", "quad")
ALONG_Z = ("quad", "place", "half")

VMEM = pl.BlockSpec(memory_space=pltpu.VMEM)
BF16, F32 = jnp.bfloat16, jnp.float32
COST = 5 * 10**10


def exchange(parts, axis):
    return lax.all_to_all(parts, axis, split_axis=0, concat_axis=0, tiled=True)


def spread(shard, axis, size):
    return exchange(jnp.broadcast_to(shard[None], (size,) + shard.shape), axis)


def swap(block, axis):
    return lax.ppermute(block, axis, [(0, 1), (1, 0)])


def along_z(block, distance):
    index = lambda z: (z % 8) * 2 + z // 8
    return lax.ppermute(block, ALONG_Z, [(index(z), index((z + distance) % 16)) for z in range(16)])


def place_on_z():
    return 8 * lax.axis_index("half") + 4 * lax.axis_index("quad") + lax.axis_index("place")


def gelu_both(preact):
    inner = gelu_coef * (preact + 0.044715 * preact * preact * preact)
    tangent = jnp.tanh(inner)
    value = 0.5 * preact * (1.0 + tangent)
    slope = 0.5 * (1.0 + tangent) + 0.5 * preact * (1.0 - tangent * tangent) * gelu_coef * (
        1.0 + 3.0 * 0.044715 * preact * preact
    )
    return value, slope


def fetch(refs, held, arrived):
    copies = [pltpu.make_async_copy(ref, to, arrived.at[i]) for i, (ref, to) in enumerate(zip(refs, held))]
    for copy in copies:
        copy.start()
    for copy in copies:
        copy.wait()


def pick_half(half, weight_in, weight_out, in_part, out_part):
    in_part[...] = weight_in[:, 128 * half : 128 * half + 128]
    for q in range(8):
        start = 256 * q + 128 * half
        out_part[64 * q : 64 * q + 64] = weight_out[:, start : start + 128]


def split_kernel(*refs):
    operands, (rows, up, down), held, arrived = refs[:5], refs[5:8], refs[8:13], refs[13]
    fetch(operands, held, arrived)
    tokens, cotangent, row_mask, weight_in, weight_out = held
    rows[0] = tokens[...]
    rows[1] = cotangent[...] * row_mask[...].astype(BF16)
    for half in range(2):

        @pl.when(lax.axis_index("half") == half)
        def _():
            pick_half(half, weight_in, weight_out, up.at[:512], up.at[512:1024])
            pick_half(1 - half, weight_in, weight_out, down.at[:512], down.at[512:1024])

    for out in (up, down):
        for which in range(2):
            for lanes in range(2):
                start = 1024 + 128 * which + 64 * lanes
                out[start : start + 64] = rows[which, :, 128 * lanes : 128 * lanes + 128]


def join_kernel(below, above, blocks, next_rows, last_rows, moved):
    copies = []
    for x in range(4):
        for at, came in ((0, below), (1024, above)):
            copies.append(pltpu.make_async_copy(came.at[:1024], blocks.at[x, at : at + 1024], moved.at[len(copies)]))
    for out, came in ((next_rows, above), (last_rows, below)):
        for which in range(2):
            for lanes in range(2):
                start = 1024 + 128 * which + 64 * lanes
                part = out.at[which, :, 128 * lanes : 128 * lanes + 128]
                copies.append(pltpu.make_async_copy(came.at[start : start + 64], part, moved.at[len(copies)]))
    for copy in copies:
        copy.start()
    for copy in copies:
        copy.wait()


def lay_rows(rows, same, ahead, behind, far):
    at_z = place_on_z()
    for offset, block in ((0, same), (1, ahead), (2, far), (15, behind)):
        for quad in range(4):
            start = lax.rem(at_z + offset + 4 * quad, 16)
            for which in range(2):
                rows[which, pl.ds(pl.multiple_of(64 * start, 64), 64)] = block[quad, which]


def lay_share(block, ins, outs):
    half = lax.div(lax.rem(place_on_z() + 12, 16), 8)
    for at, at_half in ((0, half), (1024, 1 - half)):
        for x in range(4):
            ins[pl.ds(pl.multiple_of(512 * at_half, 512), 512), 128 * x : 128 * x + 128] = block[x, at : at + 512]
            part = pl.ds(pl.multiple_of(256 * at_half + 64 * x, 64), 64)
            for q in range(8):
                start = at + 512 + 64 * q
                outs[part, 128 * q : 128 * q + 128] = block[x, start : start + 64]


def share_of(core):
    return [pl.multiple_of(512 * half + 128 * x + 64 * core, 64) for half in range(2) for x in range(4)]


def share_products(rows, ins, outs, core):
    masked = jnp.concatenate([rows[1, pl.ds(start, 64)] for start in share_of(core)], axis=0)
    contract = (((0,), (0,)), ((), ()))
    return (
        lax.dot_general(rows[0], ins[...], contract, preferred_element_type=F32),
        lax.dot_general(masked, outs[...], contract, preferred_element_type=F32),
    )


def own_kernel(same, ahead, behind, far, ins, outs, rows, preact, grad):
    lay_rows(rows, same, ahead, behind, far)
    own_preact, own_grad = share_products(rows, ins, outs, lax.axis_index("core"))
    preact[...] = own_preact.astype(BF16)
    grad[...] = own_grad


def first_kernel(rows, block, preact, grad, ins, outs, terms):
    core = lax.axis_index("core")
    lay_share(block, ins, outs)
    other_preact, other_grad = share_products(rows, ins, outs, 1 - core)
    other_preact = other_preact.astype(BF16)
    total = (grad[...] + other_grad).astype(BF16)
    for x in range(4):
        terms[x, 0, :, pl.ds(pl.multiple_of(128 * core, 128), 128)] = preact[:, 128 * x : 128 * x + 128]
        terms[x, 0, :, pl.ds(pl.multiple_of(128 * (1 - core), 128), 128)] = other_preact[:, 128 * x : 128 * x + 128]
        terms[x, 1] = total[:, 256 * x : 256 * x + 256]


def middle_kernel(terms, hidden):
    preact = sum(terms[part, 0].astype(F32) for part in range(4))
    grad = sum(terms[part, 1].astype(F32) for part in range(4))
    value, slope = gelu_both(preact)
    value = value.astype(BF16)
    grad = (grad * slope).astype(BF16)
    for part in range(4):
        hidden[part, 0] = value
        hidden[part, 1] = grad


def second_kernel(hidden, own_ins, own_outs, other_ins, other_outs, same, ahead, behind, far_a, far_b, rows):
    core, place = lax.axis_index("core"), lax.axis_index("place")
    contract = (((1,), (1,)), ((), ()))
    block = jnp.concatenate([hidden[x, 0] for x in range(4)], axis=1)
    grad = jnp.zeros((1024, 256), F32)
    for at_core, ins, outs in ((core, own_ins, own_outs), (1 - core, other_ins, other_outs)):
        product = lax.dot_general(outs[...], block, contract, preferred_element_type=F32).astype(BF16)
        for i, start in enumerate(share_of(at_core)):
            rows[0, pl.ds(start, 64)] = product[64 * i : 64 * i + 64]
        lanes = pl.ds(pl.multiple_of(128 * at_core, 128), 128)
        part = jnp.concatenate([hidden[x, 1, :, lanes] for x in range(4)], axis=1)
        grad += lax.dot_general(ins[...], part, contract, preferred_element_type=F32)
    rows[1] = grad.astype(BF16)
    for group in range(4):
        for which in range(2):
            for offset, out, slot in (
                (0, same, group),
                (1, ahead, group),
                (3, behind, group),
                (2, far_a if group < 2 else far_b, group % 2),
            ):
                at = lax.rem(place + offset, 4)
                out[slot, which] = rows[which, pl.ds(pl.multiple_of(256 * group + 64 * at, 64), 64)]


def call(kernel, shapes, *operands, scratch=(), space=VMEM, out_space=VMEM, mib=20, cost=None):
    return pl.pallas_call(
        kernel,
        out_shape=[jax.ShapeDtypeStruct(shape, BF16) if isinstance(shape, tuple) else shape for shape in shapes],
        in_specs=[space] * len(operands),
        out_specs=[out_space] * len(shapes),
        scratch_shapes=[pltpu.VMEM(shape, BF16) if isinstance(shape, tuple) else shape for shape in scratch],
        cost_estimate=pl.CostEstimate(flops=cost, bytes_accessed=0, transcendentals=0) if cost else None,
        compiler_params=pltpu.CompilerParams(vmem_limit_bytes=mib * 2**20),
    )(*operands)


def shards(tokens, weight_in, weight_out, cotangent, row_mask):
    weights = (weight_in, weight_out.T)
    operands = (tokens.T, cotangent.T, row_mask[None]) + weights
    held = lambda arrays: [pltpu.VMEM(a.shape, a.dtype) for a in arrays] + [pltpu.SemaphoreType.DMA((len(arrays),))]
    outside = pl.BlockSpec(memory_space=pl.ANY)
    own, up, down = call(
        split_kernel, [(2, 64, 256), (1280, 128), (1280, 128)], *operands,
        scratch=held(operands), space=outside, mib=60,
    )
    blocks, next_rows, last_rows = call(
        join_kernel, [(4, 2048, 128), (2, 64, 256), (2, 64, 256)], along_z(up, 4), along_z(down, -4),
        scratch=[pltpu.SemaphoreType.DMA((16,))], space=outside, out_space=outside, mib=52,
    )
    blocks = exchange(blocks, "x")
    same = jnp.stack([own, next_rows, along_z(next_rows, -4), last_rows])
    behind, ahead = along_z(same, 1), along_z(same, -1)
    far = along_z(same, -2)
    share = [(1024, 512), (512, 1024)]
    ins, outs = call(lay_share, share, blocks, cost=COST)
    rows, preact, grad = call(
        own_kernel,
        [(2, 1024, 256), (256, 512), jax.ShapeDtypeStruct((256, 1024), F32)],
        same, ahead, behind, far, ins, outs,
    )
    other_ins, other_outs, terms = call(
        first_kernel, share + [(4, 2, 256, 256)], rows, swap(blocks, "core"), preact, grad
    )
    (hidden,) = call(middle_kernel, [(4, 2, 256, 256)], exchange(terms, "y"))
    hidden = exchange(hidden, "y")
    whole, part = (4, 2, 64, 256), (2, 2, 64, 256)
    same, ahead, behind, far_a, far_b = call(
        second_kernel, [whole, whole, whole, part, part], hidden, ins, outs, other_ins, other_outs,
        scratch=[(2, 1024, 256)],
    )
    sums = [along_z(ahead, 1), along_z(behind, -1), jnp.concatenate([along_z(far_a, 2), along_z(far_b, -2)])]
    terms = same.astype(F32) + sum(block.astype(F32) for block in sums)
    terms = exchange(terms.astype(BF16), QUADS).astype(F32).sum(0)
    outs = (own.astype(F32) + terms).astype(BF16)
    return outs[0].T, outs[1].T


def solution(mesh):
    return jax.shard_map(
        shards,
        mesh=Mesh(mesh.devices.reshape(SIZES), AXES),
        in_specs=(P(IA, KA + JA), P(KA, JA + IA), P(JA, KA + IA), P(IA, KA + JA), P(IA)),
        out_specs=(P(IA, KA + JA), P(IA, KA + JA)),
        check_vma=False,
    )
```
